256 devices in a mesh: seg: 8 (over x, y_hi), space: 32 (over z, y_lo, core).
Axes of the slice: x: 4, y: 4 (y_hi: 2, y_lo: 2; y = y_hi * 2 + y_lo), z: 8, core: 2. Of those that a mesh axis runs over, the one named last changes fastest.
Arguments:
- initial_states: float32 [8, 256, 512], P('seg', 'space'), may hold values from -6 to 6
- w_lift: bfloat16 [3, 3, 1, 32], replicated, may hold values from -2.1 to 2.1
- w_second: bfloat16 [3, 3, 32, 32], replicated, may hold values from -0.7 to 0.7
- w_third: bfloat16 [3, 3, 32, 32], replicated, may hold values from -0.7 to 0.7
- w_project: bfloat16 [3, 3, 32, 1], replicated, may hold values from -0.63 to 0.63
- shift_cells: int32 [8], P('seg'), may hold values from 0 to 511
- wavenumber: int32 [2], replicated, may hold values from 1 to 31
Outputs:
- updated: float32 [8, 256, 512], P('seg', 'space')
- mismatch: float32 [8, 256, 512], P('seg', 'space')
The draws below stay inside these ranges and needn't reach their ends.
Inputs may be any that keep to these rules, and one draw needn't show every extreme that they name: `shift_cells`: column shifts between consecutive segments.
All inputs are finite; a program needn't handle non-finite values.
Results may differ from the reference program's by a relative error of at most 0.015.
Values may be sent and summed in bfloat16 or wider, within the bound.
No kernel may reach another device: no remote copies, remote signals or barrier semaphores. Data moves between devices by JAX's collectives and lax.ppermute only.
A program may use at most 64 MiB of HBM per device.

```python
import math
import jax
import jax.numpy as jnp
from jax import lax

CH = 32
STEPS = 2
COLS = 512
SEGMENTS = 8
NY = 256


leak_factor = 0.1


def channel_groups(key):
    order = jax.random.permutation(jax.random.fold_in(key, 101), CH)
    return jnp.where(order < CH // 2, 1.0, 0.0).astype(jnp.float32)


def row_profiles():
    rising = jnp.array([leak_factor, leak_factor, 1.0], jnp.float32)
    falling = jnp.array([1.0, leak_factor, leak_factor], jnp.float32)
    return (rising, falling)


def draw_w_lift(key, part):
    shape = (3, 3, 1, CH)
    sub_key = jax.random.fold_in(key, 11)
    raw = jnp.clip(jax.random.normal(sub_key, shape, jnp.float32), -3.5, 3.5)
    upward = channel_groups(key)
    rising, falling = row_profiles()
    factor = rising[:, None, None, None] * upward[None, None, None, :] + falling[:, None, None, None] * (1.0 - upward[None, None, None, :])
    return (0.6 * raw * factor).astype(jnp.bfloat16)


def hidden_kernel(key, salt):
    shape = (3, 3, CH, CH)
    sub_key = jax.random.fold_in(key, salt)
    raw = jnp.clip(jax.random.normal(sub_key, shape, jnp.float32), -3.5, 3.5)
    upward = channel_groups(key)
    rising, falling = row_profiles()
    both_up = upward[:, None] * upward[None, :]
    both_down = (1.0 - upward[:, None]) * (1.0 - upward[None, :])
    crossed = 1.0 - both_up - both_down
    factor = rising[:, None, None, None] * both_up[None, None] + falling[:, None, None, None] * both_down[None, None] + leak_factor * crossed[None, None]
    return 0.2 * raw * factor


def draw_w_second(key, part):
    return hidden_kernel(key, 22).astype(jnp.bfloat16)


def draw_w_third(key, part):
    return hidden_kernel(key, 33).astype(jnp.bfloat16)


def draw_w_project(key, part):
    shape = (3, 3, CH, 1)
    sub_key = jax.random.fold_in(key, 44)
    raw = jnp.clip(jax.random.normal(sub_key, shape, jnp.float32), -3.5, 3.5)
    upward = channel_groups(key)
    rising, falling = row_profiles()
    factor = rising[:, None, None, None] * upward[None, None, :, None] + falling[:, None, None, None] * (1.0 - upward[None, None, :, None])
    return (0.18 * raw * factor).astype(jnp.bfloat16)


def set_ends(values, key, least, top_value):
    longest = values.shape.index(max(values.shape))
    spots = []
    for shift in (0, 1):
        where = [jax.random.randint(jax.random.fold_in(key, axis), (), 0, length) for axis, length in enumerate(values.shape)]
        where[longest] = (where[longest] + shift) % values.shape[longest]
        spots.append(tuple(where))
    return values.at[spots[0]].set(least).at[spots[1]].set(top_value)


def level_of(own_key, shape, shards, smallest, top_value):
    loudness, own = 1.0, jax.random.fold_in(own_key, 6)
    for axis_at, blocks in shards:
        draws = jnp.exp(jax.random.uniform(jax.random.fold_in(own, axis_at), (blocks,), jnp.float32, smallest / len(shards), top_value / len(shards)))
        loudness = loudness * jnp.repeat(draws, shape[axis_at] // blocks).reshape([-1 if axis == axis_at else 1 for axis in range(len(shape))])
    return loudness


def noise(key, dims, spread, limit, cuts=(), kind=jnp.bfloat16):
    level = level_of(key, dims, cuts, -0.22, 0.18) if cuts else 1.0
    values = jax.random.normal(key, dims, jnp.float32) * spread * level
    return jnp.minimum(jnp.maximum(values, -limit), limit).astype(kind)


def setup_inputs(seed: int = 0) -> dict:
    seeds = jax.random.split(jax.random.key(seed), 8)
    return {
        "initial_states": noise(seeds[0], (SEGMENTS, NY, COLS), 1.0, 6.0, ((0, 8), (1, 32)), jnp.float32),
        "w_lift": draw_w_lift(jax.random.fold_in(seeds[7], 71), 0),
        "w_second": draw_w_second(jax.random.fold_in(seeds[7], 71), 0),
        "w_third": draw_w_third(jax.random.fold_in(seeds[7], 71), 0),
        "w_project": draw_w_project(jax.random.fold_in(seeds[7], 71), 0),
        "shift_cells": set_ends(jax.random.randint(seeds[5], (SEGMENTS,), 0, COLS), jax.random.fold_in(seeds[5], 1), 0, COLS - 1).astype(jnp.int32),
        "wavenumber": jax.random.randint(seeds[6], (2,), 1, NY // 8).astype(jnp.int32),
    }


time_step = 0.4
drag_rate = 0.1
learn_rate = 0.5


def correlate(padded, kernel):
    height = padded.shape[1] - 2
    widened = padded.astype(jnp.float32)
    summed = jnp.zeros((kernel.shape[3], height, padded.shape[2]), jnp.float32)
    for offset_row in range(3):
        stripe = widened[:, offset_row:offset_row + height]
        for offset_col in range(3):
            rolled = jnp.roll(stripe, 1 - offset_col, axis=2)
            summed = summed + jnp.einsum('co,crj->orj', kernel[offset_row, offset_col].astype(jnp.float32), rolled)
    return summed


def reverse_kernel(kernel):
    return jnp.transpose(kernel[::-1, ::-1], (0, 1, 3, 2))


def wrap_rows(field):
    return jnp.concatenate([field[:, -1:], field, field[:, :1]], axis=1)


def roll_each(fields, offsets):
    return jax.vmap(lambda field, offset: jnp.roll(field, offset, axis=1))(fields, offsets)


def advance(vorticity, forcing, kernels):
    activation = vorticity[None].astype(jnp.bfloat16)
    stored = []
    for layer_index in range(3):
        activation = jnp.tanh(correlate(wrap_rows(activation), kernels[layer_index])).astype(jnp.bfloat16)
        stored.append(activation)
    tendency = correlate(wrap_rows(activation), kernels[3])[0]
    return vorticity + time_step * (tendency + forcing - drag_rate * vorticity), stored


def retreat(adjoint, stored, kernels):
    cotangent = (time_step * adjoint)[None].astype(jnp.bfloat16)
    for layer_index in (3, 2, 1):
        pulled = correlate(wrap_rows(cotangent), reverse_kernel(kernels[layer_index]))
        hidden = stored[layer_index - 1].astype(jnp.float32)
        cotangent = (pulled * (1.0 - hidden * hidden)).astype(jnp.bfloat16)
    pulled = correlate(wrap_rows(cotangent), reverse_kernel(kernels[0]))[0]
    return adjoint * (1.0 - time_step * drag_rate) + pulled


def reference(initial_states, w_lift, w_second, w_third, w_project, shift_cells, wavenumber):
    kernels = (w_lift, w_second, w_third, w_project)
    row_ids = jnp.arange(NY, dtype=jnp.int32)
    phase_first = ((wavenumber[0] * row_ids) % NY).astype(jnp.float32)
    phase_second = ((wavenumber[1] * row_ids) % NY).astype(jnp.float32)
    forcing = (jnp.cos(2.0 * math.pi * phase_first / NY) + 0.5 * jnp.sin(2.0 * math.pi * phase_second / NY))[:, None]

    def integrate(start):
        vorticity = start
        for section in range(STEPS):
            vorticity, stored = advance(vorticity, forcing, kernels)
        return vorticity

    end_states = lax.map(integrate, initial_states)
    targets = roll_each(jnp.roll(initial_states, -1, axis=0), shift_cells)
    mismatch = end_states - targets

    def pull_back(pair):
        start, residual = pair
        vorticity = start
        history = []
        for section in range(STEPS):
            vorticity, stored = advance(vorticity, forcing, kernels)
            history.append(stored)
        adjoint = residual
        for section in range(STEPS - 1, -1, -1):
            adjoint = retreat(adjoint, history[section], kernels)
        return adjoint

    adjoint_start = lax.map(pull_back, (initial_states, mismatch))
    preceding = jnp.roll(roll_each(mismatch, -shift_cells), 1, axis=0)
    updated = initial_states - learn_rate * (adjoint_start - preceding)
    return updated, mismatch
```

```python
import functools
import math

import jax
import jax.numpy as jnp
from jax import lax
from jax.experimental import pallas as pl
from jax.experimental.pallas import tpu as pltpu
from jax.sharding import PartitionSpec as P


time_step = 0.4
drag_rate = 0.1
learn_rate = 0.5

ROWS = 8
LANES = 128
COLS = 512
f32 = jnp.float32
bf16 = jnp.bfloat16


def groups_of(count, most=4):
    start = 0
    while start < count:
        size = min(most, count - start)
        yield start, size
        start += size


def slot_iota(shape):
    return lax.broadcasted_iota(jnp.int32, shape, len(shape) - 2)


def widened(field):
    slot = slot_iota(field.shape)
    moved = pltpu.roll(field, 4, 0)
    left = pltpu.roll(moved, 1, 1)
    right = pltpu.roll(moved, LANES - 1, 1)
    zero = jnp.zeros_like(field)
    return jnp.where((slot >= 1) & (slot <= 4), field, jnp.where(slot == 0, left, jnp.where(slot == 5, right, zero)))


def folded(partial):
    slot = slot_iota(partial.shape)
    moved = pltpu.roll(partial, 4, 0)
    left = pltpu.roll(moved, LANES - 1, 1)
    right = pltpu.roll(moved, 1, 1)
    return partial + jnp.where(slot == 4, left, jnp.where(slot == 1, right, jnp.zeros_like(partial)))


def put(dst, row, values):
    cut = values.reshape(2, 4 * 32, LANES)
    dst[row : row + 2, 32:160, :] = cut.astype(bf16)
    before = pltpu.roll(cut[:, 96:128].reshape(64, LANES), 1, 1)
    after = pltpu.roll(cut[:, 0:32].reshape(64, LANES), LANES - 1, 1)
    dst[row : row + 2, 0:32, :] = before.astype(bf16).reshape(2, 32, LANES)
    dst[row : row + 2, 160:192, :] = after.astype(bf16).reshape(2, 32, LANES)


def set_lift(x0, rows):
    for pair in range(len(rows) // 2):
        both = jnp.concatenate([widened(rows[2 * pair]), widened(rows[2 * pair + 1])], axis=0)
        x0[16 * pair : 16 * pair + 16, :] = both.astype(bf16)


def lift(x0, dst, weight, out_rows, finish):
    for start, size in groups_of(out_rows // 2):
        x = jnp.concatenate([x0[16 * (start + g) : 16 * (start + g) + 32, :] for g in range(size)], axis=1)
        y = jnp.dot(weight, x, preferred_element_type=f32)
        for g in range(size):
            row = 2 * (start + g)
            put(dst, row, finish(y[:, g * LANES : (g + 1) * LANES], row))


def hidden(src, dst, weight, out_rows, finish):
    for start, size in groups_of(out_rows // 2):
        x = jnp.concatenate(
            [src[2 * (start + g) : 2 * (start + g) + 4].reshape(768, LANES) for g in range(size)], axis=1
        )
        y = jnp.dot(weight[...], x, preferred_element_type=f32)
        for g in range(size):
            row = 2 * (start + g)
            put(dst, row, finish(y[:, g * LANES : (g + 1) * LANES], row))


def project(src, weight, in_rows):
    parts = []
    for start, size in groups_of(in_rows // 2):
        x = jnp.concatenate(
            [src[2 * (start + g) : 2 * (start + g) + 2, 32:160, :].reshape(256, LANES) for g in range(size)], axis=1
        )
        y = jnp.dot(weight, x, preferred_element_type=f32)
        parts += [y[:, g * LANES : (g + 1) * LANES] for g in range(size)]
    rows = []
    for row in range(1, in_rows - 1):
        pair, odd = divmod(row, 2)
        if odd:
            total = parts[pair][16:24] + parts[pair + 1][0:8]
        else:
            total = parts[pair][8:16] + parts[pair - 1][24:32]
        rows.append(folded(total))
    return rows


def split3(x):
    hi = x.astype(bf16)
    rest = x - hi.astype(f32)
    mid = rest.astype(bf16)
    low = (rest - mid.astype(f32)).astype(bf16)
    return jnp.concatenate([hi, mid, low], axis=0)


def permuted(x, perm):
    rows = x.shape[0]
    y = jnp.dot(split3(x), perm, preferred_element_type=f32)
    return (y[:rows] + y[rows : 2 * rows]) + y[2 * rows :]


def split_perm(shift):
    x = lax.broadcasted_iota(jnp.int32, (COLS, COLS), 0)
    place = lax.broadcasted_iota(jnp.int32, (COLS, COLS), 1)
    column = 4 * (place & 127) + (place >> 7)
    return jnp.where(((x - column + shift) & 511) == 0, 1.0, 0.0).astype(bf16)


def join_perm(shift):
    place = lax.broadcasted_iota(jnp.int32, (COLS, COLS), 0)
    x = lax.broadcasted_iota(jnp.int32, (COLS, COLS), 1)
    column = 4 * (place & 127) + (place >> 7)
    return jnp.where(((x - column + shift) & 511) == 0, 1.0, 0.0).astype(bf16)


def store_split(dst, first, values):
    rows = values.shape[0]
    for s in range(4):
        dst[first : first + rows, 1 + s, :] = values[:, s * LANES : (s + 1) * LANES]


def joined(src, rows):
    return jnp.concatenate([src[0:rows, 1 + s, :] for s in range(4)], axis=1)


def kernel(
    shift_ref, force_ref, m2, m1, own, p1, p2, after, before, wide_ref, narrow_ref, out_ref,
    updated_ref, mismatch_ref,
    nat, field, target, prior, x0, wide, a1, a2, a3, b1, b2, b3, g1, g2, g3, fields,
):
    for layer in range(4):
        base = wide_ref[layer].astype(f32)
        for p in range(8):
            offset = 192 * (p // 4) + 32 * (p % 4)
            moved = base if offset == 0 else pltpu.roll(base, offset, 1)
            wide[layer, 32 * p : 32 * p + 32, :] = moved.astype(bf16)
    lifts = []
    for layer in range(2):
        base = narrow_ref[layer].astype(f32)
        made = []
        for p in range(8):
            offset = 8 * (p // 4) + p % 4
            moved = base if offset == 0 else pltpu.roll(base, offset, 1)
            made.append(moved[:, 0:32])
        lifts.append(jnp.concatenate(made, axis=0).astype(bf16))
    second, third, back_third, back_second = (wide.at[i] for i in range(4))
    w_out, w_back_out = out_ref[0], out_ref[1]

    nat[0:8, :] = m2[...]
    nat[8:16, :] = m1[...]
    nat[16:24, :] = own[...]
    nat[24:32, :] = p1[...]
    nat[32:40, :] = p2[...]
    nat[40:64, :] = before[0:24, :]
    store_split(field, 0, permuted(nat[...], split_perm(0)))
    store_split(target, 0, permuted(after[...], split_perm(shift_ref[0])))

    def tanh_of(y, row):
        return jnp.tanh(y)

    def advance(rows, h1, h2, h3, first):
        count = len(rows)
        set_lift(x0, rows)
        lift(x0, h1, lifts[0], count - 2, tanh_of)
        hidden(h1, h2, second, count - 4, tanh_of)
        hidden(h2, h3, third, count - 6, tanh_of)
        pushed = project(h3, w_out, count - 6)
        return [
            w + time_step * (t + force_ref[first + r] - drag_rate * w)
            for r, (w, t) in enumerate(zip(rows[4:-4], pushed))
        ]

    def masked_by(h, offset):
        def finish(y, row):
            value = h[row + offset : row + offset + 2, 32:160, :].astype(f32).reshape(256, LANES)
            return y * (1.0 - value * value)

        return finish

    def retreat(rows, h1, h2, h3, offset):
        count = len(rows)
        set_lift(x0, [time_step * l for l in rows])
        lift(x0, g3, lifts[1], count - 2, masked_by(h3, offset))
        hidden(g3, g2, back_third, count - 4, masked_by(h2, offset + 2))
        hidden(g2, g1, back_second, count - 6, masked_by(h1, offset + 4))
        pulled = project(g1, w_back_out, count - 6)
        return [l * (1.0 - time_step * drag_rate) + t for l, t in zip(rows[4:-4], pulled)]

    start = [field[r] for r in range(40)]
    middle = advance(start, a1, a2, a3, 0)
    end = advance(middle, b1, b2, b3, 4)
    gap = [e - target[r] for r, e in enumerate(end)]
    for r in range(8):
        fields[r] = gap[8 + r]
    adjoint = retreat(gap, b1, b2, b3, 2)
    adjoint = retreat(adjoint, a1, a2, a3, 10)
    for r in range(8):
        fields[8 + r] = adjoint[r]

    preceding = [field[40 + r] for r in range(24)]
    preceding = advance(preceding, g1, g2, g3, 8)
    preceding = advance(preceding, g1, g2, g3, 12)
    for r in range(8):
        prior[r] = preceding[r]

    both = permuted(joined(fields, 16), join_perm(0))
    mismatch_ref[...] = both[0:8]
    shift_before = before[24:25, :].astype(jnp.int32)
    back = permuted(joined(prior, 8), join_perm(shift_before)) - own[...]
    updated_ref[...] = own[...] - learn_rate * (both[8:16] - back)


def hidden_base(kernel_taps):
    taps = jnp.transpose(kernel_taps, (3, 0, 1, 2)).reshape(32, 3, 96)
    return jnp.pad(taps, ((0, 0), (0, 1), (0, 96))).reshape(32, 768)


def lift_base(taps):
    taps = jnp.pad(jnp.transpose(taps, (2, 0, 1)), ((0, 0), (0, 0), (0, 5))).reshape(32, 24)
    return jnp.pad(taps, ((0, 0), (0, 104)))


def out_weight(taps):
    padded = jnp.pad(taps, ((1, 1), (3, 3), (0, 0)))
    rows = []
    for row in range(4):
        for slot in range(8):
            if slot < 6:
                rows.append(padded[3 - row : 5 - row, 5 - slot : 9 - slot, :].reshape(256))
            else:
                rows.append(jnp.zeros((256,), taps.dtype))
    return jnp.stack(rows)


def reverse_kernel(kernel_taps):
    return jnp.transpose(kernel_taps[::-1, ::-1], (0, 1, 3, 2))


def per_device(initial_states, w_lift, w_second, w_third, w_project, shift_cells, wavenumber):
    segs, strips = lax.axis_size("seg"), lax.axis_size("space")
    total_rows = ROWS * strips
    own = initial_states[0]

    def fetch(x, by_seg, by_strip):
        pairs = []
        for s in range(segs):
            for p in range(strips):
                pairs.append((((s + by_seg) % segs) * strips + (p + by_strip) % strips, s * strips + p))
        return lax.ppermute(x, ("seg", "space"), pairs)

    m2, m1, p1, p2 = (fetch(own, 0, by) for by in (-2, -1, 1, 2))
    middle = jnp.concatenate([m1, own, p1], axis=0)
    shift_row = jnp.broadcast_to(shift_cells.astype(f32)[:, None], (8, COLS))
    after = fetch(middle, 1, 0)
    before = fetch(jnp.concatenate([middle, shift_row], axis=0), -1, 0)

    row_ids = lax.axis_index("space") * ROWS + jnp.arange(32, dtype=jnp.int32) - 12
    row_ids = (row_ids + total_rows) % total_rows
    phase_first = (wavenumber[0] * row_ids % total_rows).astype(f32)
    phase_second = (wavenumber[1] * row_ids % total_rows).astype(f32)
    forcing = jnp.cos(2.0 * math.pi * phase_first / total_rows) + 0.5 * jnp.sin(
        2.0 * math.pi * phase_second / total_rows
    )
    wide = jnp.stack(
        [hidden_base(w_second), hidden_base(w_third), hidden_base(reverse_kernel(w_third)), hidden_base(reverse_kernel(w_second))]
    )
    narrow = jnp.stack([lift_base(w_lift[:, :, 0, :]), lift_base(w_project[::-1, ::-1, :, 0])])
    out = jnp.stack([out_weight(w_project[:, :, :, 0]), out_weight(w_lift[::-1, ::-1, 0, :])])

    vmem = pl.BlockSpec(memory_space=pltpu.VMEM)
    smem = pl.BlockSpec(memory_space=pltpu.SMEM)

    def hid(rows):
        return pltpu.VMEM((rows, 192, LANES), bf16)

    def fld(rows):
        return pltpu.VMEM((rows, 8, LANES), f32)

    updated, mismatch = pl.pallas_call(
        kernel,
        out_shape=[jax.ShapeDtypeStruct((ROWS, COLS), f32)] * 2,
        in_specs=[smem, smem] + [vmem] * 10,
        out_specs=[vmem, vmem],
        scratch_shapes=[
            pltpu.VMEM((64, COLS), f32), fld(64), fld(24), fld(8), pltpu.VMEM((320, LANES), bf16),
            pltpu.VMEM((4, 256, 768), bf16),
            hid(38), hid(36), hid(34), hid(30), hid(28), hid(26), hid(22), hid(22), hid(22), fld(16),
        ],
        compiler_params=pltpu.CompilerParams(vmem_limit_bytes=48 * 1024 * 1024),
    )(shift_cells, forcing, m2, m1, own, p1, p2, after, before, wide, narrow, out)
    return updated[None], mismatch[None]


def solution(mesh):
    in_specs = (P("seg", "space", None), P(), P(), P(), P(), P("seg"), P())
    out_specs = (P("seg", "space", None), P("seg", "space", None))
    return jax.shard_map(per_device, mesh=mesh, in_specs=in_specs, out_specs=out_specs, check_vma=False)
```

```python
import functools
import math

import jax
import jax.numpy as jnp
from jax import lax
from jax.experimental import pallas as pl
from jax.experimental.pallas import tpu as pltpu
from jax.sharding import PartitionSpec as P


time_step = 0.4
drag_rate = 0.1
learn_rate = 0.5

ROWS = 8
LANES = 128
COLS = 512
NY = 256
f32 = jnp.float32
bf16 = jnp.bfloat16


def groups_of(count, most=4):
    start = 0
    while start < count:
        size = min(most, count - start)
        yield start, size
        start += size


def slot_iota(shape):
    return lax.broadcasted_iota(jnp.int32, shape, len(shape) - 2)


def widened(field):
    slot = slot_iota(field.shape)
    moved = pltpu.roll(field, 4, 0)
    left = pltpu.roll(moved, 1, 1)
    right = pltpu.roll(moved, LANES - 1, 1)
    zero = jnp.zeros_like(field)
    return jnp.where((slot >= 1) & (slot <= 4), field, jnp.where(slot == 0, left, jnp.where(slot == 5, right, zero)))


def folded(partial):
    slot = slot_iota(partial.shape)
    moved = pltpu.roll(partial, 4, 0)
    left = pltpu.roll(moved, LANES - 1, 1)
    right = pltpu.roll(moved, 1, 1)
    return partial + jnp.where(slot == 4, left, jnp.where(slot == 1, right, jnp.zeros_like(partial)))


def put(dst, row, values):
    cut = values.reshape(2, 4 * 32, LANES)
    dst[row : row + 2, 32:160, :] = cut.astype(bf16)
    before = pltpu.roll(cut[:, 96:128].reshape(64, LANES), 1, 1)
    after = pltpu.roll(cut[:, 0:32].reshape(64, LANES), LANES - 1, 1)
    dst[row : row + 2, 0:32, :] = before.astype(bf16).reshape(2, 32, LANES)
    dst[row : row + 2, 160:192, :] = after.astype(bf16).reshape(2, 32, LANES)


def set_lift(x0, rows):
    for pair in range(len(rows) // 2):
        both = jnp.concatenate([widened(rows[2 * pair]), widened(rows[2 * pair + 1])], axis=0)
        x0[16 * pair : 16 * pair + 16, :] = both.astype(bf16)


def lift(x0, dst, weight, out_rows, finish):
    for start, size in groups_of(out_rows // 2):
        x = jnp.concatenate([x0[16 * (start + g) : 16 * (start + g) + 32, :] for g in range(size)], axis=1)
        y = jnp.dot(weight, x, preferred_element_type=f32)
        for g in range(size):
            row = 2 * (start + g)
            put(dst, row, finish(y[:, g * LANES : (g + 1) * LANES], row))


def hidden(src, dst, weight, out_rows, finish):
    for start, size in groups_of(out_rows // 2):
        x = jnp.concatenate(
            [src[2 * (start + g) : 2 * (start + g) + 4].reshape(768, LANES) for g in range(size)], axis=1
        )
        y = jnp.dot(weight[...], x, preferred_element_type=f32)
        for g in range(size):
            row = 2 * (start + g)
            put(dst, row, finish(y[:, g * LANES : (g + 1) * LANES], row))


def project(src, weight, in_rows):
    parts = []
    for start, size in groups_of(in_rows // 2):
        x = jnp.concatenate(
            [src[2 * (start + g) : 2 * (start + g) + 2, 32:160, :].reshape(256, LANES) for g in range(size)], axis=1
        )
        y = jnp.dot(weight, x, preferred_element_type=f32)
        parts += [y[:, g * LANES : (g + 1) * LANES] for g in range(size)]
    rows = []
    for row in range(1, in_rows - 1):
        pair, odd = divmod(row, 2)
        if odd:
            total = parts[pair][16:24] + parts[pair + 1][0:8]
        else:
            total = parts[pair][8:16] + parts[pair - 1][24:32]
        rows.append(folded(total))
    return rows


def split3(x):
    hi = x.astype(bf16)
    rest = x - hi.astype(f32)
    mid = rest.astype(bf16)
    low = (rest - mid.astype(f32)).astype(bf16)
    return jnp.concatenate([hi, mid, low], axis=0)


def permuted(x, perm):
    rows = x.shape[0]
    y = jnp.dot(split3(x), perm, preferred_element_type=f32)
    return (y[:rows] + y[rows : 2 * rows]) + y[2 * rows :]


def split_perm(shift):
    x = lax.broadcasted_iota(jnp.int32, (COLS, COLS), 0)
    place = lax.broadcasted_iota(jnp.int32, (COLS, COLS), 1)
    column = 4 * (place & 127) + (place >> 7)
    return jnp.where(((x - column + shift) & 511) == 0, 1.0, 0.0).astype(bf16)


def join_perm(shift):
    place = lax.broadcasted_iota(jnp.int32, (COLS, COLS), 0)
    x = lax.broadcasted_iota(jnp.int32, (COLS, COLS), 1)
    column = 4 * (place & 127) + (place >> 7)
    return jnp.where(((x - column + shift) & 511) == 0, 1.0, 0.0).astype(bf16)


def store_split(dst, first, values):
    rows = values.shape[0]
    for s in range(4):
        dst[first : first + rows, 1 + s, :] = values[:, s * LANES : (s + 1) * LANES]


def joined(src, rows):
    return jnp.concatenate([src[0:rows, 1 + s, :] for s in range(4)], axis=1)


def hidden_weight(base, dst, layer):
    for p in range(8):
        offset = 192 * (p // 4) + 32 * (p % 4)
        moved = base if offset == 0 else pltpu.roll(base, offset, 1)
        dst[layer, 32 * p : 32 * p + 32, :] = moved.astype(bf16)


def placed(blocks):
    gap = jnp.zeros((32, 96), f32)
    parts = []
    for a in range(3):
        parts += [blocks[3 * a], blocks[3 * a + 1], blocks[3 * a + 2], gap]
    return jnp.concatenate(parts + [gap, gap], axis=1)


def chosen(taps, index, flip):
    total = jnp.where(index == (8 if flip else 0), taps[0], 0.0)
    for t in range(1, 9):
        total = jnp.where(index == (8 - t if flip else t), taps[t], total)
    return total


def tap_index(a, b):
    return jnp.where((a >= 0) & (a <= 2) & (b >= 0) & (b <= 2), 3 * a + b, -1)


def rows_and_columns(ref):
    values = ref[...].astype(f32)
    rows = [values[t // 3, t % 3 : t % 3 + 1, :] for t in range(9)]
    at = lax.broadcasted_iota(jnp.int32, (32, 32), 0)
    total = jnp.zeros((32, 32), f32)
    for t in range(9):
        total = jnp.where(at == t, jnp.broadcast_to(rows[t], (32, 32)), total)
    turned = total.T
    return rows, [turned[:, t : t + 1] for t in range(9)]


def weights_kernel(
    place, number_hbm, shift_hbm, lift_hbm, second_hbm, third_hbm, project_hbm, wide, narrow, out, force, split, join,
    split_next, join_next, number, shift, lift_ref, second, third, project_ref, sems,
):
    pairs = (
        (number_hbm, number), (shift_hbm, shift), (lift_hbm, lift_ref), (project_hbm, project_ref),
        (second_hbm, second), (third_hbm, third),
    )
    copies = [pltpu.make_async_copy(src, dst, sems.at[i]) for i, (src, dst) in enumerate(pairs)]
    for copy in copies:
        copy.start()
    split[...] = split_perm(0)
    join[...] = join_perm(0)
    for copy in copies:
        copy.wait()
    split_next[...] = split_perm(shift[0])
    join_next[...] = join_perm(shift[0])
    row = place[0] + lax.broadcasted_iota(jnp.int32, (32, LANES), 0)
    first = ((number[0] * row) & (NY - 1)).astype(f32)
    other = ((number[1] * row) & (NY - 1)).astype(f32)
    force[...] = jnp.cos(2.0 * math.pi * first / NY) + 0.5 * jnp.sin(2.0 * math.pi * other / NY)
    for layer, taps in ((0, second), (1, third)):
        hidden_weight(placed([taps[t // 3, t % 3].astype(f32).T for t in range(9)]), wide, layer)
    for layer, taps in ((2, third), (3, second)):
        hidden_weight(placed([taps[2 - t // 3, 2 - t % 3].astype(f32) for t in range(9)]), wide, layer)

    lift_rows, lift_cols = rows_and_columns(lift_ref)
    project_rows, project_cols = rows_and_columns(project_ref)
    for layer, cols, flip in ((0, lift_cols, False), (1, project_cols, True)):
        lane = lax.broadcasted_iota(jnp.int32, (32, LANES), 1)
        taps = [jnp.broadcast_to(col, (32, LANES)) for col in cols]
        for p in range(8):
            index = jnp.where(lane < 32, tap_index((lane >> 3) - p // 4, (lane & 7) - p % 4), -1)
            narrow[layer, 32 * p : 32 * p + 32, :] = chosen(taps, index, flip).astype(bf16)

    row = lax.broadcasted_iota(jnp.int32, (32, 256), 0)
    lane = lax.broadcasted_iota(jnp.int32, (32, 256), 1)
    index = jnp.where((row & 7) < 6, tap_index((lane >> 7) - (row >> 3) + 2, ((lane >> 5) & 3) - (row & 7) + 2), -1)
    for layer, rows, flip in ((0, project_rows, False), (1, lift_rows, True)):
        taps = [jnp.broadcast_to(jnp.concatenate([r] * 8, axis=1), (32, 256)) for r in rows]
        out[layer] = chosen(taps, index, flip).astype(bf16)


def tanh_of(y, row):
    return jnp.tanh(y)


def advance(rows, x0, h1, h2, h3, weights, force, first):
    count = len(rows)
    wide, narrow, out = weights
    set_lift(x0, rows)
    lift(x0, h1, narrow[0, :, 0:32], count - 2, tanh_of)
    hidden(h1, h2, wide.at[0], count - 4, tanh_of)
    hidden(h2, h3, wide.at[1], count - 6, tanh_of)
    pushed = project(h3, out[0], count - 6)
    return [
        w + time_step * (t + force[first + r : first + r + 1, :] - drag_rate * w)
        for r, (w, t) in enumerate(zip(rows[4:-4], pushed))
    ]


def masked_by(h, offset):
    def finish(y, row):
        value = h[row + offset : row + offset + 2, 32:160, :].astype(f32).reshape(256, LANES)
        return y * (1.0 - value * value)

    return finish


def retreat(rows, x0, history, made, weights, offset):
    count = len(rows)
    wide, narrow, out = weights
    (h1, h2, h3), (g1, g2, g3) = history, made
    set_lift(x0, [time_step * l for l in rows])
    lift(x0, g3, narrow[1, :, 0:32], count - 2, masked_by(h3, offset))
    hidden(g3, g2, wide.at[2], count - 4, masked_by(h2, offset + 2))
    hidden(g2, g1, wide.at[3], count - 6, masked_by(h1, offset + 4))
    pulled = project(g1, out[1], count - 6)
    return [l * (1.0 - time_step * drag_rate) + t for l, t in zip(rows[4:-4], pulled)]


def forward_kernel(m2, m1, own, p1, p2, wide, narrow, out, force, split, end, a1, a2, a3, b1, b2, b3, nat, field, x0):
    nat[0:8, :] = m2[...]
    nat[8:16, :] = m1[...]
    nat[16:24, :] = own[...]
    nat[24:32, :] = p1[...]
    nat[32:40, :] = p2[...]
    store_split(field, 0, permuted(nat[...], split[...]))
    weights = (wide, narrow, out)
    middle = advance([field[r] for r in range(40)], x0, a1, a2, a3, weights, force, 0)
    for r, row in enumerate(advance(middle, x0, b1, b2, b3, weights, force, 4)):
        end[r] = row


def gap_kernel(end, after, split_next, join_next, gap, back, target, fields):
    store_split(target, 0, permuted(after[...], split_next[...]))
    for r in range(24):
        gap[r] = end[r] - target[r]
    for r in range(8):
        fields[r] = gap[8 + r]
    back[...] = permuted(joined(fields, 8), join_next[...])


def adjoint_kernel(
    gap, a1, a2, a3, b1, b2, b3, wide, narrow, out, join, adjoint, mismatch, x0, g1, g2, g3, fields
):
    weights = (wide, narrow, out)
    rows = [gap[r] for r in range(24)]
    for r in range(8):
        fields[r] = rows[8 + r]
    rows = retreat(rows, x0, (b1, b2, b3), (g1, g2, g3), weights, 2)
    rows = retreat(rows, x0, (a1, a2, a3), (g1, g2, g3), weights, 10)
    for r in range(8):
        fields[8 + r] = rows[r]
    both = permuted(joined(fields, 16), join[...])
    mismatch[...] = both[0:8]
    adjoint[...] = both[8:16]


def per_device(initial_states, w_lift, w_second, w_third, w_project, shift_cells, wavenumber):
    segs, strips = lax.axis_size("seg"), lax.axis_size("space")
    total_rows = ROWS * strips
    own = initial_states[0]

    def fetch(x, by_seg, by_strip):
        pairs = []
        for s in range(segs):
            for p in range(strips):
                pairs.append((((s + by_seg) % segs) * strips + (p + by_strip) % strips, s * strips + p))
        return lax.ppermute(x, ("seg", "space"), pairs)

    m2, m1, p1, p2 = (fetch(own, 0, by) for by in (-2, -1, 1, 2))
    after = fetch(jnp.concatenate([m1, own, p1], axis=0), 1, 0)

    vmem = pl.BlockSpec(memory_space=pltpu.VMEM)
    smem = pl.BlockSpec(memory_space=pltpu.SMEM)

    def hid(rows):
        return pltpu.VMEM((rows, 192, LANES), bf16)

    def fld(rows):
        return pltpu.VMEM((rows, 8, LANES), f32)

    def params(mib):
        return pltpu.CompilerParams(vmem_limit_bytes=mib * 1024 * 1024)

    def cost(us):
        return pl.CostEstimate(flops=int(us * 1000000000), bytes_accessed=1000, transcendentals=0)

    nat = jax.ShapeDtypeStruct((ROWS, COLS), f32)
    x0 = pltpu.VMEM((320, LANES), bf16)
    place = lax.axis_index("space") * ROWS + total_rows - 12
    hbm = pl.BlockSpec(memory_space=pl.ANY)
    perm = pltpu.VMEM((COLS, COLS), bf16)
    wide, narrow, out, force, split, join, split_next, join_next = pl.pallas_call(
        weights_kernel,
        out_shape=[
            pltpu.VMEM((4, 256, 768), bf16), pltpu.VMEM((2, 256, LANES), bf16), pltpu.VMEM((2, 32, 256), bf16),
            pltpu.VMEM((32, LANES), f32), perm, perm, perm, perm,
        ],
        in_specs=[smem] + [hbm] * 6,
        out_specs=[vmem] * 8,
        scratch_shapes=[
            pltpu.SMEM((2,), jnp.int32), pltpu.SMEM((1,), jnp.int32), pltpu.VMEM((3, 3, 32), bf16),
            pltpu.VMEM((3, 3, 32, 32), bf16), pltpu.VMEM((3, 3, 32, 32), bf16), pltpu.VMEM((3, 3, 32), bf16),
            pltpu.SemaphoreType.DMA((6,)),
        ],
        cost_estimate=cost(2),
        compiler_params=params(56),
    )(place.astype(jnp.int32)[None], wavenumber, shift_cells, w_lift.reshape(3, 3, 32), w_second, w_third, w_project.reshape(3, 3, 32))

    end, *history = pl.pallas_call(
        forward_kernel,
        out_shape=[fld(24), hid(38), hid(36), hid(34), hid(30), hid(28), hid(26)],
        in_specs=[vmem] * 10,
        out_specs=[vmem] * 7,
        scratch_shapes=[pltpu.VMEM((40, COLS), f32), fld(40), x0],
        cost_estimate=cost(6),
        compiler_params=params(8),
    )(m2, m1, own, p1, p2, wide, narrow, out, force, split)

    gap, back = pl.pallas_call(
        gap_kernel,
        out_shape=[fld(24), pltpu.VMEM((ROWS, COLS), f32)],
        in_specs=[vmem] * 4,
        out_specs=[vmem] * 2,
        scratch_shapes=[fld(24), fld(8)],
        cost_estimate=cost(1),
        compiler_params=params(8),
    )(end, after, split_next, join_next)
    preceding = fetch(back, -1, 0)

    adjoint, mismatch = pl.pallas_call(
        adjoint_kernel,
        out_shape=[pltpu.VMEM((ROWS, COLS), f32), nat],
        in_specs=[vmem] * 11,
        out_specs=[vmem] * 2,
        scratch_shapes=[x0, hid(22), hid(22), hid(22), fld(16)],
        cost_estimate=cost(4),
        compiler_params=params(12),
    )(gap, *history, wide, narrow, out, join)
    updated = own - learn_rate * (adjoint - preceding)
    return updated[None], mismatch[None]


def solution(mesh):
    in_specs = (P("seg", "space", None), P(), P(), P(), P(), P("seg"), P())
    out_specs = (P("seg", "space", None), P("seg", "space", None))
    return jax.shard_map(per_device, mesh=mesh, in_specs=in_specs, out_specs=out_specs, check_vma=False)
```

```python
import functools
import math

import jax
import jax.numpy as jnp
from jax import lax
from jax.experimental import pallas as pl
from jax.experimental.pallas import tpu as pltpu
from jax.sharding import PartitionSpec as P


time_step = 0.4
drag_rate = 0.1
learn_rate = 0.5

ROWS = 8
LANES = 128
COLS = 512
NY = 256
f32 = jnp.float32
bf16 = jnp.bfloat16


def groups_of(count, most=2):
    start = 0
    while start < count:
        size = min(most, count - start)
        yield start, size
        start += size


def slot_iota(shape):
    return lax.broadcasted_iota(jnp.int32, shape, len(shape) - 2)


def widened(field):
    slot = slot_iota(field.shape)
    moved = pltpu.roll(field, 4, 0)
    left = pltpu.roll(moved, 1, 1)
    right = pltpu.roll(moved, LANES - 1, 1)
    zero = jnp.zeros_like(field)
    return jnp.where((slot >= 1) & (slot <= 4), field, jnp.where(slot == 0, left, jnp.where(slot == 5, right, zero)))


def folded(partial):
    slot = slot_iota(partial.shape)
    moved = pltpu.roll(partial, 4, 0)
    left = pltpu.roll(moved, LANES - 1, 1)
    right = pltpu.roll(moved, 1, 1)
    return partial + jnp.where(slot == 4, left, jnp.where(slot == 1, right, jnp.zeros_like(partial)))


def put(dst, row, values):
    cut = values.reshape(2, 4 * 32, LANES)
    dst[row : row + 2, 32:160, :] = cut.astype(bf16)
    before = pltpu.roll(cut[:, 96:128].reshape(64, LANES), 1, 1)
    after = pltpu.roll(cut[:, 0:32].reshape(64, LANES), LANES - 1, 1)
    dst[row : row + 2, 0:32, :] = before.astype(bf16).reshape(2, 32, LANES)
    dst[row : row + 2, 160:192, :] = after.astype(bf16).reshape(2, 32, LANES)


def set_lift(x0, rows):
    for pair in range(len(rows) // 2):
        both = jnp.concatenate([widened(rows[2 * pair]), widened(rows[2 * pair + 1])], axis=0)
        x0[16 * pair : 16 * pair + 16, :] = both.astype(bf16)


def lift(x0, dst, weight, out_rows, finish):
    for start, size in groups_of(out_rows // 2):
        x = jnp.concatenate([x0[16 * (start + g) : 16 * (start + g) + 32, :] for g in range(size)], axis=1)
        y = jnp.dot(weight, x, preferred_element_type=f32)
        for g in range(size):
            row = 2 * (start + g)
            put(dst, row, finish(y[:, g * LANES : (g + 1) * LANES], row))


def hidden(src, dst, weight, out_rows, finish):
    for start, size in groups_of(out_rows // 2):
        x = jnp.concatenate(
            [src[2 * (start + g) : 2 * (start + g) + 4].reshape(768, LANES) for g in range(size)], axis=1
        )
        y = jnp.dot(weight[...], x, preferred_element_type=f32)
        for g in range(size):
            row = 2 * (start + g)
            put(dst, row, finish(y[:, g * LANES : (g + 1) * LANES], row))


def project(src, weight, in_rows):
    parts = []
    for start, size in groups_of(in_rows // 2):
        x = jnp.concatenate(
            [src[2 * (start + g) : 2 * (start + g) + 2, 32:160, :].reshape(256, LANES) for g in range(size)], axis=1
        )
        y = jnp.dot(weight, x, preferred_element_type=f32)
        parts += [y[:, g * LANES : (g + 1) * LANES] for g in range(size)]
    rows = []
    for row in range(1, in_rows - 1):
        pair, odd = divmod(row, 2)
        if odd:
            total = parts[pair][16:24] + parts[pair + 1][0:8]
        else:
            total = parts[pair][8:16] + parts[pair - 1][24:32]
        rows.append(folded(total))
    return rows


def split3(x):
    hi = x.astype(bf16)
    rest = x - hi.astype(f32)
    mid = rest.astype(bf16)
    low = (rest - mid.astype(f32)).astype(bf16)
    return jnp.concatenate([hi, mid, low], axis=0)


def permuted(x, perm):
    rows = x.shape[0]
    y = jnp.dot(split3(x), perm, preferred_element_type=f32)
    return (y[:rows] + y[rows : 2 * rows]) + y[2 * rows :]


def split_perm(shift):
    x = lax.broadcasted_iota(jnp.int32, (COLS, COLS), 0)
    place = lax.broadcasted_iota(jnp.int32, (COLS, COLS), 1)
    column = 4 * (place & 127) + (place >> 7)
    return jnp.where(((x - column + shift) & 511) == 0, 1.0, 0.0).astype(bf16)


def join_perm(shift):
    place = lax.broadcasted_iota(jnp.int32, (COLS, COLS), 0)
    x = lax.broadcasted_iota(jnp.int32, (COLS, COLS), 1)
    column = 4 * (place & 127) + (place >> 7)
    return jnp.where(((x - column + shift) & 511) == 0, 1.0, 0.0).astype(bf16)


def store_split(dst, first, values):
    rows = values.shape[0]
    for s in range(4):
        dst[first : first + rows, 1 + s, :] = values[:, s * LANES : (s + 1) * LANES]


def joined(src, rows):
    return jnp.concatenate([src[0:rows, 1 + s, :] for s in range(4)], axis=1)


def hidden_weight(base, dst, layer):
    for p in range(8):
        offset = 192 * (p // 4) + 32 * (p % 4)
        moved = base if offset == 0 else pltpu.roll(base, offset, 1)
        dst[layer, 32 * p : 32 * p + 32, :] = moved.astype(bf16)


def placed(blocks):
    gap = jnp.zeros((32, 96), f32)
    parts = []
    for a in range(3):
        parts += [blocks[3 * a], blocks[3 * a + 1], blocks[3 * a + 2], gap]
    return jnp.concatenate(parts + [gap, gap], axis=1)


def chosen(taps, index, flip):
    total = jnp.where(index == (8 if flip else 0), taps[0], 0.0)
    for t in range(1, 9):
        total = jnp.where(index == (8 - t if flip else t), taps[t], total)
    return total


def tap_index(a, b):
    return jnp.where((a >= 0) & (a <= 2) & (b >= 0) & (b <= 2), 3 * a + b, -1)


def rows_and_columns(ref):
    values = ref[...].astype(f32)
    rows = [values[t // 3, t % 3 : t % 3 + 1, :] for t in range(9)]
    at = lax.broadcasted_iota(jnp.int32, (32, 32), 0)
    total = jnp.zeros((32, 32), f32)
    for t in range(9):
        total = jnp.where(at == t, jnp.broadcast_to(rows[t], (32, 32)), total)
    turned = total.T
    return rows, [turned[:, t : t + 1] for t in range(9)]


def weights_kernel(
    code, number_hbm, shift_hbm, lift_hbm, second_hbm, third_hbm, project_hbm, wide, narrow, out, force, split, join,
    split_next, join_next, number, shift, lift_ref, second, third, project_ref, sems,
):
    pairs = (
        (number_hbm, number), (shift_hbm, shift), (lift_hbm, lift_ref), (project_hbm, project_ref),
        (second_hbm, second), (third_hbm, third),
    )
    copies = [pltpu.make_async_copy(src, dst, sems.at[i]) for i, (src, dst) in enumerate(pairs)]
    for copy in copies:
        copy.start()
    split[...] = split_perm(0)
    join[...] = join_perm(0)
    for copy in copies:
        copy.wait()
    split_next[...] = split_perm(shift[0])
    join_next[...] = join_perm(shift[0])
    row = ROWS * (code[0] & 31) + NY - 12 + lax.broadcasted_iota(jnp.int32, (32, LANES), 0)
    first = ((number[0] * row) & (NY - 1)).astype(f32)
    other = ((number[1] * row) & (NY - 1)).astype(f32)
    force[...] = jnp.cos(2.0 * math.pi * first / NY) + 0.5 * jnp.sin(2.0 * math.pi * other / NY)
    for layer, taps in ((0, second), (1, third)):
        hidden_weight(placed([taps[t // 3, t % 3].astype(f32).T for t in range(9)]), wide, layer)
    for layer, taps in ((2, third), (3, second)):
        hidden_weight(placed([taps[2 - t // 3, 2 - t % 3].astype(f32) for t in range(9)]), wide, layer)

    lift_rows, lift_cols = rows_and_columns(lift_ref)
    project_rows, project_cols = rows_and_columns(project_ref)
    for layer, cols, flip in ((0, lift_cols, False), (1, project_cols, True)):
        lane = lax.broadcasted_iota(jnp.int32, (32, LANES), 1)
        taps = [jnp.broadcast_to(col, (32, LANES)) for col in cols]
        for p in range(8):
            index = jnp.where(lane < 32, tap_index((lane >> 3) - p // 4, (lane & 7) - p % 4), -1)
            narrow[layer, 32 * p : 32 * p + 32, :] = chosen(taps, index, flip).astype(bf16)

    row = lax.broadcasted_iota(jnp.int32, (32, 256), 0)
    lane = lax.broadcasted_iota(jnp.int32, (32, 256), 1)
    index = jnp.where((row & 7) < 6, tap_index((lane >> 7) - (row >> 3) + 2, ((lane >> 5) & 3) - (row & 7) + 2), -1)
    for layer, rows, flip in ((0, project_rows, False), (1, lift_rows, True)):
        taps = [jnp.broadcast_to(jnp.concatenate([r] * 8, axis=1), (32, 256)) for r in rows]
        out[layer] = chosen(taps, index, flip).astype(bf16)


def tanh_of(y, row):
    return jnp.tanh(y)


def advance(rows, x0, h1, h2, h3, weights, force, first):
    count = len(rows)
    wide, narrow, out = weights
    set_lift(x0, rows)
    lift(x0, h1, narrow[0, :, 0:32], count - 2, tanh_of)
    hidden(h1, h2, wide.at[0], count - 4, tanh_of)
    hidden(h2, h3, wide.at[1], count - 6, tanh_of)
    pushed = project(h3, out[0], count - 6)
    return [
        w + time_step * (t + force[first + r : first + r + 1, :] - drag_rate * w)
        for r, (w, t) in enumerate(zip(rows[4:-4], pushed))
    ]


def masked_by(h, offset):
    def finish(y, row):
        value = h[row + offset : row + offset + 2, 32:160, :].astype(f32).reshape(256, LANES)
        return y * (1.0 - value * value)

    return finish


def retreat(rows, x0, history, made, weights, offset):
    count = len(rows)
    wide, narrow, out = weights
    (h1, h2, h3), (g1, g2, g3) = history, made
    set_lift(x0, [time_step * l for l in rows])
    lift(x0, g3, narrow[1, :, 0:32], count - 2, masked_by(h3, offset))
    hidden(g3, g2, wide.at[2], count - 4, masked_by(h2, offset + 2))
    hidden(g2, g1, wide.at[3], count - 6, masked_by(h1, offset + 4))
    pulled = project(g1, out[1], count - 6)
    return [l * (1.0 - time_step * drag_rate) + t for l, t in zip(rows[4:-4], pulled)]


def by_strip(code, within, across):
    even = (code[0] & 1) == 0
    return jnp.where(even, across, within), jnp.where(even, within, across)


def forward_kernel(
    code, m2, within, own, across, p2, wide, narrow, out, force, split, end, a1, a2, a3, b1, b2, b3, nat, field, x0
):
    m1, p1 = by_strip(code, within[...], across[...])
    nat[0:8, :] = m2[...]
    nat[8:16, :] = m1
    nat[16:24, :] = own[...]
    nat[24:32, :] = p1
    nat[32:40, :] = p2[...]
    store_split(field, 0, permuted(nat[...], split[...]))
    weights = (wide, narrow, out)
    middle = advance([field[r] for r in range(40)], x0, a1, a2, a3, weights, force, 0)
    for r, row in enumerate(advance(middle, x0, b1, b2, b3, weights, force, 4)):
        end[r] = row


def gap_kernel(code, end, after, split_next, join_next, gap, back, nat, target, fields):
    below, above = by_strip(code, after[0:8, :], after[16:24, :])
    nat[0:8, :] = below
    nat[8:16, :] = after[8:16, :]
    nat[16:24, :] = above
    store_split(target, 0, permuted(nat[...], split_next[...]))
    for r in range(24):
        gap[r] = end[r] - target[r]
    for r in range(8):
        fields[r] = gap[8 + r]
    back[...] = permuted(joined(fields, 8), join_next[...])


def adjoint_kernel(
    gap, a1, a2, a3, b1, b2, b3, wide, narrow, out, join, adjoint, mismatch, x0, g1, g2, g3, fields, gap_rows, sem
):
    weights = (wide, narrow, out)
    rows = [gap[r] for r in range(24)]
    for r in range(8):
        fields[r] = rows[8 + r]
    gap_rows[...] = permuted(joined(fields, 8), join[...])
    copy = pltpu.make_async_copy(gap_rows, mismatch, sem)
    copy.start()
    rows = retreat(rows, x0, (b1, b2, b3), (g1, g2, g3), weights, 2)
    rows = retreat(rows, x0, (a1, a2, a3), (g1, g2, g3), weights, 10)
    for r in range(8):
        fields[8 + r] = rows[r]
    adjoint[...] = permuted(joined(fields.at[8:16], 8), join[...])
    copy.wait()


def per_device(initial_states, w_lift, w_second, w_third, w_project, shift_cells, wavenumber):
    segs, strips = lax.axis_size("seg"), lax.axis_size("space")
    own = initial_states[0]

    def moved(x, source):
        pairs = []
        for s in range(segs):
            for p in range(strips):
                from_seg, from_strip = source(s, p)
                pairs.append((from_seg % segs * strips + from_strip % strips, s * strips + p))
        return lax.ppermute(x, ("seg", "space"), pairs)

    m2 = moved(own, lambda s, p: (s, p - 2))
    across = moved(own, lambda s, p: (s, p - 1 if p % 2 == 0 else p + 1))
    p2 = moved(own, lambda s, p: (s, p + 2))
    within = moved(own, lambda s, p: (s, p + 1 if p % 2 == 0 else p - 1))
    within, m2, across, p2 = lax.optimization_barrier((within, m2, across, p2))
    after = moved(jnp.concatenate([within, own, across], axis=0), lambda s, p: (s + 1, p))

    vmem = pl.BlockSpec(memory_space=pltpu.VMEM)
    smem = pl.BlockSpec(memory_space=pltpu.SMEM)

    def hid(rows):
        return pltpu.VMEM((rows, 192, LANES), bf16)

    def fld(rows):
        return pltpu.VMEM((rows, 8, LANES), f32)

    def params(mib):
        return pltpu.CompilerParams(vmem_limit_bytes=mib * 1024 * 1024)

    def cost(us):
        return pl.CostEstimate(flops=int(us * 1000000000), bytes_accessed=1000, transcendentals=0)

    nat = jax.ShapeDtypeStruct((ROWS, COLS), f32)
    x0 = pltpu.VMEM((320, LANES), bf16)
    code = (lax.axis_index("seg") * strips + lax.axis_index("space")).astype(jnp.int32)[None]
    hbm = pl.BlockSpec(memory_space=pl.ANY)
    perm = pltpu.VMEM((COLS, COLS), bf16)
    wide, narrow, out, force, split, join, split_next, join_next = pl.pallas_call(
        weights_kernel,
        out_shape=[
            pltpu.VMEM((4, 256, 768), bf16), pltpu.VMEM((2, 256, LANES), bf16), pltpu.VMEM((2, 32, 256), bf16),
            pltpu.VMEM((32, LANES), f32), perm, perm, perm, perm,
        ],
        in_specs=[smem] + [hbm] * 6,
        out_specs=[vmem] * 8,
        scratch_shapes=[
            pltpu.SMEM((2,), jnp.int32), pltpu.SMEM((1,), jnp.int32), pltpu.VMEM((3, 3, 32), bf16),
            pltpu.VMEM((3, 3, 32, 32), bf16), pltpu.VMEM((3, 3, 32, 32), bf16), pltpu.VMEM((3, 3, 32), bf16),
            pltpu.SemaphoreType.DMA((6,)),
        ],
        cost_estimate=cost(2),
        compiler_params=params(56),
    )(code, wavenumber, shift_cells, w_lift.reshape(3, 3, 32), w_second, w_third, w_project.reshape(3, 3, 32))

    end, *history = pl.pallas_call(
        forward_kernel,
        out_shape=[fld(24), hid(38), hid(36), hid(34), hid(30), hid(28), hid(26)],
        in_specs=[smem] + [vmem] * 10,
        out_specs=[vmem] * 7,
        scratch_shapes=[pltpu.VMEM((40, COLS), f32), fld(40), x0],
        cost_estimate=cost(6),
        compiler_params=params(8),
    )(code, m2, within, own, across, p2, wide, narrow, out, force, split)

    gap, back = pl.pallas_call(
        gap_kernel,
        out_shape=[fld(24), pltpu.VMEM((ROWS, COLS), f32)],
        in_specs=[smem] + [vmem] * 4,
        out_specs=[vmem] * 2,
        scratch_shapes=[pltpu.VMEM((24, COLS), f32), fld(24), fld(8)],
        cost_estimate=cost(1),
        compiler_params=params(8),
    )(code, end, after, split_next, join_next)
    preceding = moved(back, lambda s, p: (s - 1, p))

    adjoint, mismatch = pl.pallas_call(
        adjoint_kernel,
        out_shape=[pltpu.VMEM((ROWS, COLS), f32), nat],
        in_specs=[vmem] * 11,
        out_specs=[vmem, pl.BlockSpec(memory_space=pl.ANY)],
        scratch_shapes=[
            x0, hid(22), hid(22), hid(22), fld(16), pltpu.VMEM((ROWS, COLS), f32), pltpu.SemaphoreType.DMA,
        ],
        cost_estimate=cost(4),
        compiler_params=params(12),
    )(gap, *history, wide, narrow, out, join)
    updated = own - learn_rate * (adjoint - preceding)
    return updated[None], mismatch[None]


def solution(mesh):
    in_specs = (P("seg", "space", None), P(), P(), P(), P(), P("seg"), P())
    out_specs = (P("seg", "space", None), P("seg", "space", None))
    return jax.shard_map(per_device, mesh=mesh, in_specs=in_specs, out_specs=out_specs, check_vma=False)
```

```python
import functools
import math

import jax
import jax.numpy as jnp
from jax import lax
from jax.experimental import pallas as pl
from jax.experimental.pallas import tpu as pltpu
from jax.sharding import PartitionSpec as P


time_step = 0.4
drag_rate = 0.1
learn_rate = 0.5

ROWS = 8
LANES = 128
COLS = 512
NY = 256
f32 = jnp.float32
bf16 = jnp.bfloat16


def groups_of(count, most=2):
    start = 0
    while start < count:
        size = min(most, count - start)
        yield start, size
        start += size


def slot_iota(shape):
    return lax.broadcasted_iota(jnp.int32, shape, len(shape) - 2)


def widened(field):
    slot = slot_iota(field.shape)
    moved = pltpu.roll(field, 4, 0)
    left = pltpu.roll(moved, 1, 1)
    right = pltpu.roll(moved, LANES - 1, 1)
    zero = jnp.zeros_like(field)
    return jnp.where((slot >= 1) & (slot <= 4), field, jnp.where(slot == 0, left, jnp.where(slot == 5, right, zero)))


def folded(partial):
    slot = slot_iota(partial.shape)
    moved = pltpu.roll(partial, 4, 0)
    left = pltpu.roll(moved, LANES - 1, 1)
    right = pltpu.roll(moved, 1, 1)
    return partial + jnp.where(slot == 4, left, jnp.where(slot == 1, right, jnp.zeros_like(partial)))


def put(dst, row, values):
    cut = values.reshape(2, 4 * 32, LANES)
    dst[row : row + 2, 32:160, :] = cut.astype(bf16)
    before = pltpu.roll(cut[:, 96:128].reshape(64, LANES), 1, 1)
    after = pltpu.roll(cut[:, 0:32].reshape(64, LANES), LANES - 1, 1)
    dst[row : row + 2, 0:32, :] = before.astype(bf16).reshape(2, 32, LANES)
    dst[row : row + 2, 160:192, :] = after.astype(bf16).reshape(2, 32, LANES)


def set_lift(x0, rows):
    for pair in range(len(rows) // 2):
        both = jnp.concatenate([widened(rows[2 * pair]), widened(rows[2 * pair + 1])], axis=0)
        x0[16 * pair : 16 * pair + 16, :] = both.astype(bf16)


def lift(x0, dst, weight, out_rows, finish):
    for start, size in groups_of(out_rows // 2):
        x = jnp.concatenate([x0[16 * (start + g) : 16 * (start + g) + 32, :] for g in range(size)], axis=1)
        y = jnp.dot(weight, x, preferred_element_type=f32)
        for g in range(size):
            row = 2 * (start + g)
            put(dst, row, finish(y[:, g * LANES : (g + 1) * LANES], row))


def hidden(src, dst, weight, out_rows, finish):
    for start, size in groups_of(out_rows // 2):
        x = jnp.concatenate(
            [src[2 * (start + g) : 2 * (start + g) + 4].reshape(768, LANES) for g in range(size)], axis=1
        )
        y = jnp.dot(weight[...], x, preferred_element_type=f32)
        for g in range(size):
            row = 2 * (start + g)
            put(dst, row, finish(y[:, g * LANES : (g + 1) * LANES], row))


def project(src, weight, in_rows):
    parts = []
    for start, size in groups_of(in_rows // 2):
        x = jnp.concatenate(
            [src[2 * (start + g) : 2 * (start + g) + 2, 32:160, :].reshape(256, LANES) for g in range(size)], axis=1
        )
        y = jnp.dot(weight, x, preferred_element_type=f32)
        parts += [y[:, g * LANES : (g + 1) * LANES] for g in range(size)]
    rows = []
    for row in range(1, in_rows - 1):
        pair, odd = divmod(row, 2)
        if odd:
            total = parts[pair][16:24] + parts[pair + 1][0:8]
        else:
            total = parts[pair][8:16] + parts[pair - 1][24:32]
        rows.append(folded(total))
    return rows


def split3(x):
    hi = x.astype(bf16)
    rest = x - hi.astype(f32)
    mid = rest.astype(bf16)
    low = (rest - mid.astype(f32)).astype(bf16)
    return jnp.concatenate([hi, mid, low], axis=0)


def permuted(x, perm):
    rows = x.shape[0]
    y = jnp.dot(split3(x), perm, preferred_element_type=f32)
    return (y[:rows] + y[rows : 2 * rows]) + y[2 * rows :]


def split_perm(shift):
    x = lax.broadcasted_iota(jnp.int32, (COLS, COLS), 0)
    place = lax.broadcasted_iota(jnp.int32, (COLS, COLS), 1)
    column = 4 * (place & 127) + (place >> 7)
    return jnp.where(((x - column + shift) & 511) == 0, 1.0, 0.0).astype(bf16)


def join_perm(shift):
    place = lax.broadcasted_iota(jnp.int32, (COLS, COLS), 0)
    x = lax.broadcasted_iota(jnp.int32, (COLS, COLS), 1)
    column = 4 * (place & 127) + (place >> 7)
    return jnp.where(((x - column + shift) & 511) == 0, 1.0, 0.0).astype(bf16)


def store_split(dst, first, values):
    rows = values.shape[0]
    for s in range(4):
        dst[first : first + rows, 1 + s, :] = values[:, s * LANES : (s + 1) * LANES]


def joined(src, rows):
    return jnp.concatenate([src[0:rows, 1 + s, :] for s in range(4)], axis=1)


def hidden_weight(base, dst, layer):
    for p in range(8):
        offset = 192 * (p // 4) + 32 * (p % 4)
        moved = base if offset == 0 else pltpu.roll(base, offset, 1)
        dst[layer, 32 * p : 32 * p + 32, :] = moved.astype(bf16)


def placed(blocks):
    gap = jnp.zeros((32, 96), f32)
    parts = []
    for a in range(3):
        parts += [blocks[3 * a], blocks[3 * a + 1], blocks[3 * a + 2], gap]
    return jnp.concatenate(parts + [gap, gap], axis=1)


def chosen(taps, index, flip):
    total = jnp.where(index == (8 if flip else 0), taps[0], 0.0)
    for t in range(1, 9):
        total = jnp.where(index == (8 - t if flip else t), taps[t], total)
    return total


def tap_index(a, b):
    return jnp.where((a >= 0) & (a <= 2) & (b >= 0) & (b <= 2), 3 * a + b, -1)


def rows_and_columns(ref):
    values = ref[...].astype(f32)
    rows = [values[t // 3, t % 3 : t % 3 + 1, :] for t in range(9)]
    at = lax.broadcasted_iota(jnp.int32, (32, 32), 0)
    total = jnp.zeros((32, 32), f32)
    for t in range(9):
        total = jnp.where(at == t, jnp.broadcast_to(rows[t], (32, 32)), total)
    turned = total.T
    return rows, [turned[:, t : t + 1] for t in range(9)]


def lift_weight(cols, flip, dst):
    lane = lax.broadcasted_iota(jnp.int32, (32, LANES), 1)
    taps = [jnp.broadcast_to(col, (32, LANES)) for col in cols]
    for p in range(8):
        index = jnp.where(lane < 32, tap_index((lane >> 3) - p // 4, (lane & 7) - p % 4), -1)
        dst[32 * p : 32 * p + 32, :] = chosen(taps, index, flip).astype(bf16)


def out_weight(rows, flip):
    row = lax.broadcasted_iota(jnp.int32, (32, 256), 0)
    lane = lax.broadcasted_iota(jnp.int32, (32, 256), 1)
    index = jnp.where((row & 7) < 6, tap_index((lane >> 7) - (row >> 3) + 2, ((lane >> 5) & 3) - (row & 7) + 2), -1)
    taps = [jnp.broadcast_to(jnp.concatenate([r] * 8, axis=1), (32, 256)) for r in rows]
    return chosen(taps, index, flip).astype(bf16)


def weights_kernel(
    number_hbm, shift_hbm, lift_hbm, second_hbm, third_hbm, project_hbm,
    wide, narrow, out, force, split, split_next, join_next, lift_ref, second, third, project_ref,
    number, shift, sems,
):
    pairs = (
        (number_hbm, number), (shift_hbm, shift), (lift_hbm, lift_ref), (project_hbm, project_ref),
        (second_hbm, second), (third_hbm, third),
    )
    copies = [pltpu.make_async_copy(src, dst, sems.at[i]) for i, (src, dst) in enumerate(pairs)]
    for copy in copies:
        copy.start()
    split[...] = split_perm(0)
    for copy in copies[2:]:
        copy.wait()
    for layer, taps in ((0, second), (1, third)):
        hidden_weight(placed([taps[t // 3, t % 3].astype(f32).T for t in range(9)]), wide, layer)
    lift_weight(rows_and_columns(lift_ref)[1], False, narrow)
    out[...] = out_weight(rows_and_columns(project_ref)[0], False)
    for copy in copies[:2]:
        copy.wait()
    split_next[...] = split_perm(shift[0])
    join_next[...] = join_perm(shift[0])
    row = ROWS * lax.axis_index("space") + NY - 12 + lax.broadcasted_iota(jnp.int32, (32, LANES), 0)
    first = ((number[0] * row) & (NY - 1)).astype(f32)
    other = ((number[1] * row) & (NY - 1)).astype(f32)
    force[...] = jnp.cos(2.0 * math.pi * first / NY) + 0.5 * jnp.sin(2.0 * math.pi * other / NY)


def tanh_of(y, row):
    return jnp.tanh(y)


def advance(rows, x0, h1, h2, h3, weights, force, first):
    count = len(rows)
    wide, narrow, out = weights
    set_lift(x0, rows)
    lift(x0, h1, narrow[:, 0:32], count - 2, tanh_of)
    hidden(h1, h2, wide.at[0], count - 4, tanh_of)
    hidden(h2, h3, wide.at[1], count - 6, tanh_of)
    pushed = project(h3, out[...], count - 6)
    return [
        w + time_step * (t + force[first + r : first + r + 1, :] - drag_rate * w)
        for r, (w, t) in enumerate(zip(rows[4:-4], pushed))
    ]


def masked_by(h, offset):
    def finish(y, row):
        value = h[row + offset : row + offset + 2, 32:160, :].astype(f32).reshape(256, LANES)
        return y * (1.0 - value * value)

    return finish


def retreat(rows, x0, history, made, weights, offset, between=None):
    count = len(rows)
    wide, narrow, out = weights
    (h1, h2, h3), (g1, g2, g3) = history, made
    set_lift(x0, [time_step * l for l in rows])
    lift(x0, g3, narrow[:, 0:32], count - 2, masked_by(h3, offset))
    if between is not None:
        between()
    hidden(g3, g2, wide.at[0], count - 4, masked_by(h2, offset + 2))
    hidden(g2, g1, wide.at[1], count - 6, masked_by(h1, offset + 4))
    pulled = project(g1, out[...], count - 6)
    return [l * (1.0 - time_step * drag_rate) + t for l, t in zip(rows[4:-4], pulled)]


def by_strip(within, across):
    even = lax.rem(lax.axis_index("space"), 2) == 0
    return jnp.where(even, across, within), jnp.where(even, within, across)


def forward_kernel(
    m2, within, own, across, p2, wide, narrow, out, force, split, end, a1, a2, a3, b1, b2, b3, nat, field, x0
):
    m1, p1 = by_strip(within[...], across[...])
    nat[0:8, :] = m2[...]
    nat[8:16, :] = m1
    nat[16:24, :] = own[...]
    nat[24:32, :] = p1
    nat[32:40, :] = p2[...]
    store_split(field, 0, permuted(nat[...], split[...]))
    weights = (wide, narrow, out)
    middle = advance([field[r] for r in range(40)], x0, a1, a2, a3, weights, force, 0)
    for r, row in enumerate(advance(middle, x0, b1, b2, b3, weights, force, 4)):
        end[r] = row


def gap_kernel(end, after, split_next, join_next, gap, back, nat, target, fields):
    below, above = by_strip(after[0:8, :], after[16:24, :])
    nat[0:8, :] = below
    nat[8:16, :] = after[8:16, :]
    nat[16:24, :] = above
    store_split(target, 0, permuted(nat[...], split_next[...]))
    for r in range(24):
        gap[r] = end[r] - target[r]
    for r in range(8):
        fields[r] = gap[8 + r]
    back[...] = permuted(joined(fields, 8), join_next[...])


def adjoint_kernel(
    gap, a1, a2, a3, b1, b2, b3, lift_ref, second, third, project_ref, adjoint, mismatch,
    wide, narrow, out, join, x0, g1, g2, g3, fields, gap_rows, sem,
):
    weights = (wide, narrow, out)
    lift_weight(rows_and_columns(project_ref)[1], True, narrow)
    rows = [gap[r] for r in range(24)]
    join[...] = join_perm(0)
    for r in range(8):
        fields[r] = rows[8 + r]
    gap_rows[...] = permuted(joined(fields, 8), join[...])
    copy = pltpu.make_async_copy(gap_rows, mismatch, sem)
    copy.start()

    def build():
        for layer, taps in ((0, third), (1, second)):
            hidden_weight(placed([taps[2 - t // 3, 2 - t % 3].astype(f32) for t in range(9)]), wide, layer)
        out[...] = out_weight(rows_and_columns(lift_ref)[0], True)

    rows = retreat(rows, x0, (b1, b2, b3), (g1, g2, g3), weights, 2, build)
    rows = retreat(rows, x0, (a1, a2, a3), (g1, g2, g3), weights, 10)
    for r in range(8):
        fields[8 + r] = rows[r]
    adjoint[...] = permuted(joined(fields.at[8:16], 8), join[...])
    copy.wait()


def per_device(initial_states, w_lift, w_second, w_third, w_project, shift_cells, wavenumber):
    segs, strips = lax.axis_size("seg"), lax.axis_size("space")
    own = initial_states[0]

    def moved(x, source):
        pairs = []
        for s in range(segs):
            for p in range(strips):
                from_seg, from_strip = source(s, p)
                pairs.append((from_seg % segs * strips + from_strip % strips, s * strips + p))
        return lax.ppermute(x, ("seg", "space"), pairs)

    m2 = moved(own, lambda s, p: (s, p - 2))
    across = moved(own, lambda s, p: (s, p - 1 if p % 2 == 0 else p + 1))
    p2 = moved(own, lambda s, p: (s, p + 2))
    within = moved(own, lambda s, p: (s, p + 1 if p % 2 == 0 else p - 1))
    within, m2, across, p2 = lax.optimization_barrier((within, m2, across, p2))
    after = moved(jnp.concatenate([within, own, across], axis=0), lambda s, p: (s + 1, p))

    vmem = pl.BlockSpec(memory_space=pltpu.VMEM)

    def hid(rows):
        return pltpu.VMEM((rows, 192, LANES), bf16)

    def fld(rows):
        return pltpu.VMEM((rows, 8, LANES), f32)

    def params(mib):
        return pltpu.CompilerParams(vmem_limit_bytes=mib * 1024 * 1024)

    def cost(us):
        return pl.CostEstimate(flops=int(us * 1000000000), bytes_accessed=1000, transcendentals=0)

    nat = jax.ShapeDtypeStruct((ROWS, COLS), f32)
    x0 = pltpu.VMEM((320, LANES), bf16)
    hbm = pl.BlockSpec(memory_space=pl.ANY)
    perm = pltpu.VMEM((COLS, COLS), bf16)
    taps, hidden_taps = (3, 3, 32), (3, 3, 32, 32)
    wide_shape, narrow_shape, out_shape = (
        pltpu.VMEM((2, 256, 768), bf16), pltpu.VMEM((256, LANES), bf16), pltpu.VMEM((32, 256), bf16)
    )
    wide, narrow, out, force, split, split_next, join_next, *raw = pl.pallas_call(
        weights_kernel,
        out_shape=[
            wide_shape, narrow_shape, out_shape, pltpu.VMEM((32, LANES), f32), perm, perm, perm,
            pltpu.VMEM(taps, bf16), pltpu.VMEM(hidden_taps, bf16), pltpu.VMEM(hidden_taps, bf16), pltpu.VMEM(taps, bf16),
        ],
        in_specs=[hbm] * 6,
        out_specs=[vmem] * 11,
        scratch_shapes=[pltpu.SMEM((2,), jnp.int32), pltpu.SMEM((1,), jnp.int32), pltpu.SemaphoreType.DMA((6,))],
        cost_estimate=cost(2),
        compiler_params=params(56),
    )(wavenumber, shift_cells, w_lift.reshape(taps), w_second, w_third, w_project.reshape(taps))

    end, *history = pl.pallas_call(
        forward_kernel,
        out_shape=[fld(24), hid(38), hid(36), hid(34), hid(30), hid(28), hid(26)],
        in_specs=[vmem] * 10,
        out_specs=[vmem] * 7,
        scratch_shapes=[pltpu.VMEM((40, COLS), f32), fld(40), x0],
        cost_estimate=cost(6),
        compiler_params=params(8),
    )(m2, within, own, across, p2, wide, narrow, out, force, split)

    gap, back = pl.pallas_call(
        gap_kernel,
        out_shape=[fld(24), pltpu.VMEM((ROWS, COLS), f32)],
        in_specs=[vmem] * 4,
        out_specs=[vmem] * 2,
        scratch_shapes=[pltpu.VMEM((24, COLS), f32), fld(24), fld(8)],
        cost_estimate=cost(1),
        compiler_params=params(8),
    )(end, after, split_next, join_next)
    preceding = moved(back, lambda s, p: (s - 1, p))

    adjoint, mismatch = pl.pallas_call(
        adjoint_kernel,
        out_shape=[pltpu.VMEM((ROWS, COLS), f32), nat],
        in_specs=[vmem] * 11,
        out_specs=[vmem, pl.BlockSpec(memory_space=pl.ANY)],
        scratch_shapes=[
            wide_shape, narrow_shape, out_shape, perm,
            x0, hid(22), hid(22), hid(22), fld(16), pltpu.VMEM((ROWS, COLS), f32), pltpu.SemaphoreType.DMA,
        ],
        cost_estimate=cost(4),
        compiler_params=params(12),
    )(gap, *history, *raw)
    updated = own - learn_rate * (adjoint - preceding)
    return updated[None], mismatch[None]


def solution(mesh):
    in_specs = (P("seg", "space", None), P(), P(), P(), P(), P("seg"), P())
    out_specs = (P("seg", "space", None), P("seg", "space", None))
    return jax.shard_map(per_device, mesh=mesh, in_specs=in_specs, out_specs=out_specs, check_vma=False)
```

```python
import functools
import math

import jax
import jax.numpy as jnp
from jax import lax
from jax.experimental import pallas as pl
from jax.experimental.pallas import tpu as pltpu
from jax.sharding import PartitionSpec as P


time_step = 0.4
drag_rate = 0.1
learn_rate = 0.5

ROWS = 8
LANES = 128
COLS = 512
NY = 256
f32 = jnp.float32
bf16 = jnp.bfloat16


def groups_of(count, most=2):
    start = 0
    while start < count:
        size = min(most, count - start)
        yield start, size
        start += size


def slot_iota(shape):
    return lax.broadcasted_iota(jnp.int32, shape, len(shape) - 2)


def widened(field):
    slot = slot_iota(field.shape)
    moved = pltpu.roll(field, 4, 0)
    left = pltpu.roll(moved, 1, 1)
    right = pltpu.roll(moved, LANES - 1, 1)
    zero = jnp.zeros_like(field)
    return jnp.where((slot >= 1) & (slot <= 4), field, jnp.where(slot == 0, left, jnp.where(slot == 5, right, zero)))


def folded(partial):
    slot = slot_iota(partial.shape)
    moved = pltpu.roll(partial, 4, 0)
    left = pltpu.roll(moved, LANES - 1, 1)
    right = pltpu.roll(moved, 1, 1)
    return partial + jnp.where(slot == 4, left, jnp.where(slot == 1, right, jnp.zeros_like(partial)))


def put(dst, row, values):
    cut = values.reshape(2, 4 * 32, LANES)
    dst[row : row + 2, 32:160, :] = cut.astype(bf16)
    before = pltpu.roll(cut[:, 96:128].reshape(64, LANES), 1, 1)
    after = pltpu.roll(cut[:, 0:32].reshape(64, LANES), LANES - 1, 1)
    dst[row : row + 2, 0:32, :] = before.astype(bf16).reshape(2, 32, LANES)
    dst[row : row + 2, 160:192, :] = after.astype(bf16).reshape(2, 32, LANES)


def set_lift(x0, rows):
    for pair in range(len(rows) // 2):
        both = jnp.concatenate([widened(rows[2 * pair]), widened(rows[2 * pair + 1])], axis=0)
        x0[16 * pair : 16 * pair + 16, :] = both.astype(bf16)


def lift(x0, dst, weight, out_rows, finish):
    for start, size in groups_of(out_rows // 2):
        x = jnp.concatenate([x0[16 * (start + g) : 16 * (start + g) + 32, :] for g in range(size)], axis=1)
        y = jnp.dot(weight, x, preferred_element_type=f32)
        for g in range(size):
            row = 2 * (start + g)
            put(dst, row, finish(y[:, g * LANES : (g + 1) * LANES], row))


def hidden(src, dst, weight, out_rows, finish):
    for start, size in groups_of(out_rows // 2):
        x = jnp.concatenate(
            [src[2 * (start + g) : 2 * (start + g) + 4].reshape(768, LANES) for g in range(size)], axis=1
        )
        y = jnp.dot(weight[...], x, preferred_element_type=f32)
        for g in range(size):
            row = 2 * (start + g)
            put(dst, row, finish(y[:, g * LANES : (g + 1) * LANES], row))


def project(src, weight, in_rows):
    parts = []
    for start, size in groups_of(in_rows // 2):
        x = jnp.concatenate(
            [src[2 * (start + g) : 2 * (start + g) + 2, 32:160, :].reshape(256, LANES) for g in range(size)], axis=1
        )
        y = jnp.dot(weight, x, preferred_element_type=f32)
        parts += [y[:, g * LANES : (g + 1) * LANES] for g in range(size)]
    rows = []
    for row in range(1, in_rows - 1):
        pair, odd = divmod(row, 2)
        if odd:
            total = parts[pair][16:24] + parts[pair + 1][0:8]
        else:
            total = parts[pair][8:16] + parts[pair - 1][24:32]
        rows.append(folded(total))
    return rows


def split3(x):
    hi = x.astype(bf16)
    rest = x - hi.astype(f32)
    mid = rest.astype(bf16)
    low = (rest - mid.astype(f32)).astype(bf16)
    return jnp.concatenate([hi, mid, low], axis=0)


def permuted(x, perm):
    rows = x.shape[0]
    y = jnp.dot(split3(x), perm, preferred_element_type=f32)
    return (y[:rows] + y[rows : 2 * rows]) + y[2 * rows :]


def split_perm(shift):
    x = lax.broadcasted_iota(jnp.int32, (COLS, COLS), 0)
    place = lax.broadcasted_iota(jnp.int32, (COLS, COLS), 1)
    column = 4 * (place & 127) + (place >> 7)
    return jnp.where(((x - column + shift) & 511) == 0, 1.0, 0.0).astype(bf16)


def join_perm(shift):
    place = lax.broadcasted_iota(jnp.int32, (COLS, COLS), 0)
    x = lax.broadcasted_iota(jnp.int32, (COLS, COLS), 1)
    column = 4 * (place & 127) + (place >> 7)
    return jnp.where(((x - column + shift) & 511) == 0, 1.0, 0.0).astype(bf16)


def store_split(dst, first, values):
    rows = values.shape[0]
    for s in range(4):
        dst[first : first + rows, 1 + s, :] = values[:, s * LANES : (s + 1) * LANES]


def joined(src, rows):
    return jnp.concatenate([src[0:rows, 1 + s, :] for s in range(4)], axis=1)


def hidden_weight(base, dst, layer):
    for p in range(8):
        offset = 192 * (p // 4) + 32 * (p % 4)
        moved = base if offset == 0 else pltpu.roll(base, offset, 1)
        dst[layer, 32 * p : 32 * p + 32, :] = moved.astype(bf16)


def placed(blocks):
    gap = jnp.zeros((32, 96), f32)
    parts = []
    for a in range(3):
        parts += [blocks[3 * a], blocks[3 * a + 1], blocks[3 * a + 2], gap]
    return jnp.concatenate(parts + [gap, gap], axis=1)


def chosen(taps, index, flip):
    total = jnp.where(index == (8 if flip else 0), taps[0], 0.0)
    for t in range(1, 9):
        total = jnp.where(index == (8 - t if flip else t), taps[t], total)
    return total


def tap_index(a, b):
    return jnp.where((a >= 0) & (a <= 2) & (b >= 0) & (b <= 2), 3 * a + b, -1)


def rows_and_columns(ref):
    values = ref[...].astype(f32)
    rows = [values[t // 3, t % 3 : t % 3 + 1, :] for t in range(9)]
    at = lax.broadcasted_iota(jnp.int32, (32, 32), 0)
    total = jnp.zeros((32, 32), f32)
    for t in range(9):
        total = jnp.where(at == t, jnp.broadcast_to(rows[t], (32, 32)), total)
    turned = total.T
    return rows, [turned[:, t : t + 1] for t in range(9)]


def lift_weight(cols, flip, dst):
    lane = lax.broadcasted_iota(jnp.int32, (32, LANES), 1)
    taps = [jnp.broadcast_to(col, (32, LANES)) for col in cols]
    for p in range(8):
        index = jnp.where(lane < 32, tap_index((lane >> 3) - p // 4, (lane & 7) - p % 4), -1)
        dst[32 * p : 32 * p + 32, :] = chosen(taps, index, flip).astype(bf16)


def out_weight(rows, flip):
    row = lax.broadcasted_iota(jnp.int32, (32, 256), 0)
    lane = lax.broadcasted_iota(jnp.int32, (32, 256), 1)
    index = jnp.where((row & 7) < 6, tap_index((lane >> 7) - (row >> 3) + 2, ((lane >> 5) & 3) - (row & 7) + 2), -1)
    taps = [jnp.broadcast_to(jnp.concatenate([r] * 8, axis=1), (32, 256)) for r in rows]
    return chosen(taps, index, flip).astype(bf16)


def weights_kernel(
    number_hbm, shift_hbm, lift_hbm, second_hbm, third_hbm, project_hbm,
    wide, narrow, out, force, split, split_next, join_next, lift_ref, second, third, project_ref,
    number, shift, sems,
):
    pairs = (
        (number_hbm, number), (shift_hbm, shift), (lift_hbm, lift_ref), (project_hbm, project_ref),
        (second_hbm, second), (third_hbm, third),
    )
    copies = [pltpu.make_async_copy(src, dst, sems.at[i]) for i, (src, dst) in enumerate(pairs)]
    for copy in copies:
        copy.start()
    split[...] = split_perm(0)
    for copy in copies[2:]:
        copy.wait()
    for layer, taps in ((0, second), (1, third)):
        hidden_weight(placed([taps[t // 3, t % 3].astype(f32).T for t in range(9)]), wide, layer)
    lift_weight(rows_and_columns(lift_ref)[1], False, narrow)
    out[...] = out_weight(rows_and_columns(project_ref)[0], False)
    for copy in copies[:2]:
        copy.wait()
    split_next[...] = split_perm(shift[0])
    join_next[...] = join_perm(shift[0])
    row = ROWS * lax.axis_index("space") + NY - 12 + lax.broadcasted_iota(jnp.int32, (32, LANES), 0)
    first = ((number[0] * row) & (NY - 1)).astype(f32)
    other = ((number[1] * row) & (NY - 1)).astype(f32)
    force[...] = jnp.cos(2.0 * math.pi * first / NY) + 0.5 * jnp.sin(2.0 * math.pi * other / NY)


def tanh_of(y, row):
    return jnp.tanh(y)


def advance(rows, x0, h1, h2, h3, weights, force, first):
    count = len(rows)
    wide, narrow, out = weights
    set_lift(x0, rows)
    lift(x0, h1, narrow[:, 0:32], count - 2, tanh_of)
    hidden(h1, h2, wide.at[0], count - 4, tanh_of)
    hidden(h2, h3, wide.at[1], count - 6, tanh_of)
    pushed = project(h3, out[...], count - 6)
    return [
        w + time_step * (t + force[first + r : first + r + 1, :] - drag_rate * w)
        for r, (w, t) in enumerate(zip(rows[4:-4], pushed))
    ]


def masked_by(h, offset):
    def finish(y, row):
        value = h[row + offset : row + offset + 2, 32:160, :].astype(f32).reshape(256, LANES)
        return y * (1.0 - value * value)

    return finish


def retreat(rows, x0, history, made, weights, offset, between=None):
    count = len(rows)
    wide, narrow, out = weights
    (h1, h2, h3), (g1, g2, g3) = history, made
    set_lift(x0, [time_step * l for l in rows])
    lift(x0, g3, narrow[:, 0:32], count - 2, masked_by(h3, offset))
    if between is not None:
        between()
    hidden(g3, g2, wide.at[0], count - 4, masked_by(h2, offset + 2))
    hidden(g2, g1, wide.at[1], count - 6, masked_by(h1, offset + 4))
    pulled = project(g1, out[...], count - 6)
    return [l * (1.0 - time_step * drag_rate) + t for l, t in zip(rows[4:-4], pulled)]


def by_strip(within, across):
    even = lax.rem(lax.axis_index("space"), 2) == 0
    return jnp.where(even, across, within), jnp.where(even, within, across)


def forward_kernel(
    m2, within, own, across, p2, wide, narrow, out, force, split, end, a1, a2, a3, b1, b2, b3, nat, field, x0
):
    m1, p1 = by_strip(within[...], across[...])
    nat[0:8, :] = m2[...]
    nat[8:16, :] = m1
    nat[16:24, :] = own[...]
    nat[24:32, :] = p1
    nat[32:40, :] = p2[...]
    store_split(field, 0, permuted(nat[...], split[...]))
    weights = (wide, narrow, out)
    middle = advance([field[r] for r in range(40)], x0, a1, a2, a3, weights, force, 0)
    for r, row in enumerate(advance(middle, x0, b1, b2, b3, weights, force, 4)):
        end[r] = row


def gap_kernel(end, after, split_next, join_next, gap, back, nat, target, fields):
    below, above = by_strip(after[0:8, :], after[16:24, :])
    nat[0:8, :] = below
    nat[8:16, :] = after[8:16, :]
    nat[16:24, :] = above
    store_split(target, 0, permuted(nat[...], split_next[...]))
    for r in range(24):
        gap[r] = end[r] - target[r]
    for r in range(8):
        fields[r] = gap[8 + r]
    back[...] = permuted(joined(fields, 8), join_next[...])


def adjoint_kernel(
    gap, a1, a2, a3, b1, b2, b3, lift_ref, second, third, project_ref, adjoint, mismatch,
    wide, narrow, out, join, x0, g1, g2, g3, fields, gap_rows, sem,
):
    weights = (wide, narrow, out)
    lift_weight(rows_and_columns(project_ref)[1], True, narrow)
    rows = [gap[r] for r in range(24)]
    copy = pltpu.make_async_copy(gap_rows, mismatch, sem)

    def build():
        for layer, taps in ((0, third), (1, second)):
            hidden_weight(placed([taps[2 - t // 3, 2 - t % 3].astype(f32) for t in range(9)]), wide, layer)
        out[...] = out_weight(rows_and_columns(lift_ref)[0], True)
        join[...] = join_perm(0)
        for r in range(8):
            fields[r] = gap[8 + r]
        gap_rows[...] = permuted(joined(fields, 8), join[...])
        copy.start()

    rows = retreat(rows, x0, (b1, b2, b3), (g1, g2, g3), weights, 2, build)
    rows = retreat(rows, x0, (a1, a2, a3), (g1, g2, g3), weights, 10)
    for r in range(8):
        fields[8 + r] = rows[r]
    adjoint[...] = permuted(joined(fields.at[8:16], 8), join[...])
    copy.wait()


def per_device(initial_states, w_lift, w_second, w_third, w_project, shift_cells, wavenumber):
    segs, strips = lax.axis_size("seg"), lax.axis_size("space")
    own = initial_states[0]

    def moved(x, source):
        pairs = []
        for s in range(segs):
            for p in range(strips):
                from_seg, from_strip = source(s, p)
                pairs.append((from_seg % segs * strips + from_strip % strips, s * strips + p))
        return lax.ppermute(x, ("seg", "space"), pairs)

    m2 = moved(own, lambda s, p: (s, p - 2))
    across = moved(own, lambda s, p: (s, p - 1 if p % 2 == 0 else p + 1))
    p2 = moved(own, lambda s, p: (s, p + 2))
    within = moved(own, lambda s, p: (s, p + 1 if p % 2 == 0 else p - 1))
    within, m2, across, p2 = lax.optimization_barrier((within, m2, across, p2))
    after = moved(jnp.concatenate([within, own, across], axis=0), lambda s, p: (s + 1, p))

    vmem = pl.BlockSpec(memory_space=pltpu.VMEM)

    def hid(rows):
        return pltpu.VMEM((rows, 192, LANES), bf16)

    def fld(rows):
        return pltpu.VMEM((rows, 8, LANES), f32)

    def params(mib):
        return pltpu.CompilerParams(vmem_limit_bytes=mib * 1024 * 1024)

    def cost(us):
        return pl.CostEstimate(flops=int(us * 1000000000), bytes_accessed=1000, transcendentals=0)

    nat = jax.ShapeDtypeStruct((ROWS, COLS), f32)
    x0 = pltpu.VMEM((320, LANES), bf16)
    hbm = pl.BlockSpec(memory_space=pl.ANY)
    perm = pltpu.VMEM((COLS, COLS), bf16)
    taps, hidden_taps = (3, 3, 32), (3, 3, 32, 32)
    wide_shape, narrow_shape, out_shape = (
        pltpu.VMEM((2, 256, 768), bf16), pltpu.VMEM((256, LANES), bf16), pltpu.VMEM((32, 256), bf16)
    )
    wide, narrow, out, force, split, split_next, join_next, *raw = pl.pallas_call(
        weights_kernel,
        out_shape=[
            wide_shape, narrow_shape, out_shape, pltpu.VMEM((32, LANES), f32), perm, perm, perm,
            pltpu.VMEM(taps, bf16), pltpu.VMEM(hidden_taps, bf16), pltpu.VMEM(hidden_taps, bf16), pltpu.VMEM(taps, bf16),
        ],
        in_specs=[hbm] * 6,
        out_specs=[vmem] * 11,
        scratch_shapes=[pltpu.SMEM((2,), jnp.int32), pltpu.SMEM((1,), jnp.int32), pltpu.SemaphoreType.DMA((6,))],
        cost_estimate=cost(2),
        compiler_params=params(56),
    )(wavenumber, shift_cells, w_lift.reshape(taps), w_second, w_third, w_project.reshape(taps))

    end, *history = pl.pallas_call(
        forward_kernel,
        out_shape=[fld(24), hid(38), hid(36), hid(34), hid(30), hid(28), hid(26)],
        in_specs=[vmem] * 10,
        out_specs=[vmem] * 7,
        scratch_shapes=[pltpu.VMEM((40, COLS), f32), fld(40), x0],
        cost_estimate=cost(6),
        compiler_params=params(8),
    )(m2, within, own, across, p2, wide, narrow, out, force, split)

    gap, back = pl.pallas_call(
        gap_kernel,
        out_shape=[fld(24), pltpu.VMEM((ROWS, COLS), f32)],
        in_specs=[vmem] * 4,
        out_specs=[vmem] * 2,
        scratch_shapes=[pltpu.VMEM((24, COLS), f32), fld(24), fld(8)],
        cost_estimate=cost(1),
        compiler_params=params(8),
    )(end, after, split_next, join_next)
    preceding = moved(back, lambda s, p: (s - 1, p))

    adjoint, mismatch = pl.pallas_call(
        adjoint_kernel,
        out_shape=[pltpu.VMEM((ROWS, COLS), f32), nat],
        in_specs=[vmem] * 11,
        out_specs=[vmem, pl.BlockSpec(memory_space=pl.ANY)],
        scratch_shapes=[
            wide_shape, narrow_shape, out_shape, perm,
            x0, hid(22), hid(22), hid(22), fld(16), pltpu.VMEM((ROWS, COLS), f32), pltpu.SemaphoreType.DMA,
        ],
        cost_estimate=cost(4),
        compiler_params=params(12),
    )(gap, *history, *raw)
    updated = own - learn_rate * (adjoint - preceding)
    return updated[None], mismatch[None]


def solution(mesh):
    in_specs = (P("seg", "space", None), P(), P(), P(), P(), P("seg"), P())
    out_specs = (P("seg", "space", None), P("seg", "space", None))
    return jax.shard_map(per_device, mesh=mesh, in_specs=in_specs, out_specs=out_specs, check_vma=False)
```
